512 devices in a mesh: prow: 32 (over y, z_lo, core), pcol: 16 (over z_hi, x).
Axes of the slice: x: 4, y: 8, z: 8 (z_hi: 4, z_lo: 2; z = z_hi * 2 + z_lo), core: 2. Of those that a mesh axis runs over, the one named last changes fastest.
Arguments:
- inverse_blocks: bfloat16 [24576, 24576], P('prow', 'pcol'), may hold values from -0.0390625 to 0.0390625
- lower_panel: bfloat16 [2, 24576, 384], P(None, 'prow', 'pcol'), may hold values from -0.75 to 0.75
- diag_inverse: float32 [2, 384, 384], P(None, None, 'pcol'), may hold values from -6 to 6
- structure: int32 [2, 48], replicated, may hold values from 0 to 63, all different within a row
Outputs:
- selected_column: float32 [2, 24576, 384], P(None, 'prow', 'pcol')
- diagonal_block: float32 [2, 384, 384], P(None, None, 'pcol')
The draws below stay inside these ranges and needn't reach their ends.
Inputs may be any that keep to these rules, and one draw needn't show every extreme that they name: `structure`: each row names 48 different block numbers; every block number appears in some row.
All inputs are finite; a program needn't handle non-finite values.
Results may differ from the reference program's by a relative error of at most 0.0003.
Values may be sent and summed in bfloat16 or wider, within the bound.
A program may use at most 64 MiB of HBM per device.

```python
import jax
import jax.numpy as jnp
from jax import lax

W = 384
SNODES = 2
NB = 64
SB = 48


def steps_of(own_key, dims, cuts, low, high):
    level = 1.0
    for position, shards_of in cuts:
        heights = jax.random.uniform(jax.random.fold_in(jax.random.fold_in(own_key, 6), position), (shards_of,), jnp.float32, low / len(cuts), high / len(cuts))
        level = level * jnp.repeat(jnp.exp(heights), dims[position] // shards_of).reshape((-1,) + (1,) * (len(dims) - 1 - position))
    return level


def different_ones(own_key, rows, number_of, top, lift):
    ranking = jax.random.permutation(jax.random.fold_in(own_key, 1), number_of)
    favour = ranking
    for power in range(3):
        favour = favour * favour // number_of
    favour = favour * lift // number_of
    tickets = jax.random.randint(jax.random.fold_in(own_key, 2), (rows, number_of), 0, 4096) + favour
    fixed_rows = jax.random.permutation(jax.random.fold_in(own_key, 3), rows)[jnp.arange(number_of) % rows]
    tickets = jnp.where(jnp.arange(rows)[:, None] == fixed_rows[None, :], 1 << 14, tickets)
    merit = tickets * number_of + jnp.arange(number_of)
    return lax.top_k(merit.astype(jnp.int32), top)[1].astype(jnp.int32)


def noise(stream_key, shape, deviation, most, split=(), kind=jnp.bfloat16):
    factor_of = steps_of(stream_key, shape, split, -0.22, 0.18) if split else 1.0
    array = jax.random.normal(stream_key, shape, jnp.float32) * deviation * factor_of
    return jnp.minimum(jnp.maximum(array, -most), most).astype(kind)


def setup_inputs(seed: int = 0) -> dict:
    key_list = jax.random.split(jax.random.key(seed), 5)
    inverse_blocks = noise(key_list[0], (NB * W, NB * W), (NB * W) ** -0.5, 0.0390625, ((0, 32), (1, 16)))
    lower_panel = noise(key_list[1], (SNODES, NB * W, W), 0.125, 0.75, ((1, 32), (2, 16)))
    diag_inverse = noise(key_list[2], (SNODES, W, W), 1.0, 6.0, ((2, 16),), jnp.float32)
    structure = different_ones(key_list[3], SNODES, NB, SB, 0)
    return dict(inverse_blocks=inverse_blocks, lower_panel=lower_panel, diag_inverse=diag_inverse, structure=structure)


def block_presence(structure):
    block_ids = jnp.arange(NB, dtype=jnp.int32)
    matches = (structure[:, :, None] == block_ids[None, None, :]).astype(jnp.float32)
    return jnp.minimum(jnp.sum(matches, axis=1), 1.0)


def reference(inverse_blocks, lower_panel, diag_inverse, structure):
    present = block_presence(structure)
    row_present = jnp.repeat(present, W, axis=1)
    masked = (lower_panel.astype(jnp.float32) * row_present[:, :, None]).astype(jnp.bfloat16)
    right_block = jnp.concatenate([masked[snode].astype(jnp.float32) for snode in range(SNODES)], axis=1)

    def row_block(block_index):
        row_slab = lax.dynamic_slice_in_dim(inverse_blocks, (block_index * W).astype(jnp.int32), W, 0).astype(jnp.float32)
        return jnp.dot(row_slab, right_block, precision=lax.Precision.HIGHEST)

    product = lax.map(row_block, jnp.arange(NB, dtype=jnp.int32))
    product = product.reshape(NB * W, SNODES, W).transpose(1, 0, 2)
    selected_column = -(product * row_present[:, :, None])
    correction = jnp.einsum("srw,srv->swv", masked.astype(jnp.float32), selected_column, precision=lax.Precision.HIGHEST)
    diagonal_block = diag_inverse - correction
    return selected_column, diagonal_block
```

```python
import functools

import jax
import jax.numpy as jnp
from jax import lax
from jax.experimental import pallas as pl
from jax.experimental.pallas import tpu as pltpu
from jax.sharding import PartitionSpec as P

MESH = pl.DeviceIdType.MESH
F32, BF16, I16, I32 = jnp.float32, jnp.bfloat16, jnp.int16, jnp.int32
SNODES = 2
X = 4
NT = (((1,), (1,)), ((), ()))
TINY = 1e-33


def encode(value):
    top = jnp.maximum(jnp.max(jnp.abs(value), axis=0, keepdims=True), TINY)
    code = jnp.round(value * (32767.0 / top)).astype(I32).astype(I16)
    return code, top * (1.0 / 32767.0)


def decode(code, scale):
    return code.astype(I32).astype(F32) * scale


def kernel(
    rows_n, cols_n, a_hbm, l_ref, dinv_ref, struct_ref, sel_ref, diag_ref,
    a_ref, own, panel, prod, xs, xs_scale, xr, xr_scale, acc, zs, zs_scale, zr, zr_scale,
    ts, ts_scale, tr, tr_scale, sorted_panel, dpart, dsum_in, dtile, dfin,
    a_sem, l_sem, zl_sem, sib_send, sib_recv, ring_send, ring_recv, x_send, x_recv, z_send, z_recv,
    t_sem, rs_send, rs_recv, ag_send, ag_recv,
):
    wide = l_ref.shape[1]
    rows = l_ref.shape[2]
    vb = SNODES * wide
    nq = cols_n
    y_n = rows_n // 4
    zh_n = nq // X
    half = y_n // 2
    tiles_across = nq * wide // 128
    tiles = (vb // 8) * tiles_across

    prow, q = lax.axis_index("prow"), lax.axis_index("pcol")
    p, core = prow // 2, prow % 2
    y, zl = p // 2, p % 2
    zh, x = q // X, q % X
    depth = lax.rem(y - q // 2 + y_n, y_n)
    mine = 2 * depth + (zl + q) % 2

    def row_of(yy, zz, cc):
        return lax.rem(yy + y_n, y_n) * 4 + zz * 2 + cc

    partner = (row_of(p // 2 + q // 2, (p + q) % 2, core), p)
    source = (q * 2 + core, mine)
    is_self = jnp.logical_and(partner[0] == prow, partner[1] == q)
    up, down = (row_of(y + 1, zl, core), q), (row_of(y - 1, zl, core), q)
    across = (row_of(y, 1 - zl, core), q)
    sibling = (row_of(y, zl, 1 - core), q)
    xpeer = [(prow, zh * X + lax.rem(x + o, X)) for o in range(1, X)]
    zpeer = [(prow, lax.rem(zh + o, zh_n) * X + x) for o in range(1, zh_n)]

    load_a = pltpu.make_async_copy(a_hbm, a_ref, a_sem)
    load_a.start()

    barrier = pltpu.get_barrier_semaphore()
    fixed = [up, down, across, sibling] + xpeer + zpeer
    for device in fixed:
        pl.semaphore_signal(barrier, inc=1, device_id=device, device_id_type=MESH)

    @pl.when(jnp.logical_not(is_self))
    def _():
        pl.semaphore_signal(barrier, inc=1, device_id=partner, device_id_type=MESH)
        pl.semaphore_signal(barrier, inc=1, device_id=source, device_id_type=MESH)

    lane = lax.broadcasted_iota(I32, (1, rows), 1)
    table = struct_ref[...]
    marks = []
    for s in range(SNODES):
        hits = [
            jnp.max((table[s : s + 1, :] == prow * 2 + b).astype(F32), axis=1, keepdims=True) for b in range(2)
        ]
        marks.append(jnp.where(lane < rows // 2, hits[0], hits[1]))
    mask = jnp.concatenate([jnp.broadcast_to(m, (wide, rows)) for m in marks], axis=0)
    raw = jnp.concatenate([l_ref[s].astype(F32) for s in range(SNODES)], axis=0)
    own[...] = (raw * mask).astype(BF16)

    @pl.when(is_self)
    def _():
        pl.semaphore_wait(barrier, len(fixed))

    @pl.when(jnp.logical_not(is_self))
    def _():
        pl.semaphore_wait(barrier, len(fixed) + 2)

    started = []

    def send(src, dst, send_sem, recv_sem, device):
        copy = pltpu.make_async_remote_copy(
            src_ref=src, dst_ref=dst, send_sem=send_sem, recv_sem=recv_sem, device_id=device, device_id_type=MESH
        )
        copy.start()
        started.append(copy)
        return copy

    def block(index, first=0, count=2):
        start = pl.multiple_of((lax.rem(index + y_n, y_n) * 2 + first) * vb, 16)
        return panel.at[core, pl.ds(start, count * vb), :]

    def other(index, first=0, count=2):
        start = pl.multiple_of((lax.rem(index + y_n, y_n) * 2 + first) * vb, 16)
        return panel.at[1 - core, pl.ds(start, count * vb), :]

    def slot(index):
        return panel.at[core, pl.ds(pl.multiple_of(index * vb, 16), vb), :]

    def hand_over(src, dst, sems, recv_dst):
        @pl.when(is_self)
        def _():
            copy = pltpu.make_async_copy(src, dst, sems.at[2])
            copy.start()
            copy.wait()

        @pl.when(jnp.logical_not(is_self))
        def _():
            copy = pltpu.make_async_remote_copy(
                src_ref=src, dst_ref=dst, send_sem=sems.at[0], recv_sem=sems.at[1],
                device_id=partner, device_id_type=MESH,
            )
            copy.start()
            copy.wait_send()
            pltpu.make_async_remote_copy(
                src_ref=src, dst_ref=recv_dst, send_sem=sems.at[0], recv_sem=sems.at[1],
                device_id=partner, device_id_type=MESH,
            ).wait_recv()

    hand_over(own, slot(q), l_sem, slot(mine))

    pair = send(slot(mine), slot(mine), zl_sem.at[0], zl_sem.at[1], across)
    pair.wait_recv()

    sib = []

    def to_sibling(index, first=0, count=2):
        k = len(sib)
        send(block(index, first, count), block(index, first, count), sib_send.at[k], sib_recv.at[k], sibling)
        sib.append((index, first, count))

    def wait_sibling(k):
        piece = other(*sib[k])
        pltpu.make_async_remote_copy(
            src_ref=piece, dst_ref=piece, send_sem=sib_send.at[k], recv_sem=sib_recv.at[k],
            device_id=sibling, device_id_type=MESH,
        ).wait_recv()

    def ring(t):
        part_up, part_down = ((0, 2), (0, 2)) if t < half else ((0, 1), (1, 1))
        src_up, src_down = block(depth - (t - 1), *part_up), block(depth + (t - 1), *part_down)
        send(src_up, src_up, ring_send.at[0, t - 1], ring_recv.at[0, t - 1], up)
        send(src_down, src_down, ring_send.at[1, t - 1], ring_recv.at[1, t - 1], down)

    def ring_wait(t):
        part_up, part_down = ((0, 2), (0, 2)) if t < half else ((0, 1), (1, 1))
        dst_up, dst_down = block(depth - t, *part_up), block(depth + t, *part_down)
        for way, dst, device in ((0, dst_up, up), (1, dst_down, down)):
            pltpu.make_async_remote_copy(
                src_ref=dst, dst_ref=dst, send_sem=ring_send.at[way, t - 1], recv_sem=ring_recv.at[way, t - 1],
                device_id=device, device_id_type=MESH,
            ).wait_recv()

    for t in range(1, half + 1):
        ring(t)
        if t == 1:
            to_sibling(depth)
        else:
            to_sibling(depth - (t - 1))
            to_sibling(depth + (t - 1))
        ring_wait(t)
    to_sibling(depth + half)
    for k in range(len(sib)):
        wait_sibling(k)
    load_a.wait()

    for g in range(zh_n):
        group = pl.ds(g * X * vb, X * vb)
        prod[g] = lax.dot_general(
            panel[0, group, :], a_ref[:, :rows], NT, preferred_element_type=F32
        ) + lax.dot_general(panel[1, group, :], a_ref[:, rows:], NT, preferred_element_type=F32)
        for o in range(1, X):
            to = lax.rem(x + o, X)
            code, scale = encode(prod[g, pl.ds(pl.multiple_of(to * vb, 8), vb), :])
            xs[g, o - 1] = code
            xs_scale[g, o - 1] = scale
            send(xs.at[g, o - 1], xr.at[g, o - 1], x_send.at[0, g, o - 1], x_recv.at[0, g, o - 1], xpeer[o - 1])
            send(
                xs_scale.at[g, o - 1], xr_scale.at[g, o - 1],
                x_send.at[1, g, o - 1], x_recv.at[1, g, o - 1], xpeer[o - 1],
            )

    def wait_for(dst, send_sem, recv_sem, device):
        pltpu.make_async_remote_copy(
            src_ref=dst, dst_ref=dst, send_sem=send_sem, recv_sem=recv_sem, device_id=device, device_id_type=MESH
        ).wait_recv()

    for s in range(SNODES):
        for k in range(0, nq, 2):
            pieces = [panel[core, (k + i) * vb : (k + i + 1) * vb, :].astype(F32) for i in range(2)]
            both = jnp.concatenate([piece[s * wide : (s + 1) * wide] for piece in pieces], axis=0)
            sorted_panel[s, k * wide : (k + 2) * wide, :] = both.astype(BF16)

    for g in range(zh_n):
        total = prod[g, pl.ds(pl.multiple_of(x * vb, 8), vb), :]
        for o in range(X - 1):
            wait_for(xr.at[g, o], x_send.at[0, g, o], x_recv.at[0, g, o], xpeer[o])
            wait_for(xr_scale.at[g, o], x_send.at[1, g, o], x_recv.at[1, g, o], xpeer[o])
            total = total + decode(xr[g, o], xr_scale[g, o])
        acc[g] = total

    for o in range(1, zh_n):
        code, scale = encode(acc[lax.rem(zh + o, zh_n)])
        zs[o - 1] = code
        zs_scale[o - 1] = scale
        send(zs.at[o - 1], zr.at[o - 1], z_send.at[0, o - 1], z_recv.at[0, o - 1], zpeer[o - 1])
        send(zs_scale.at[o - 1], zr_scale.at[o - 1], z_send.at[1, o - 1], z_recv.at[1, o - 1], zpeer[o - 1])
    total = acc[zh]
    for o in range(zh_n - 1):
        wait_for(zr.at[o], z_send.at[0, o], z_recv.at[0, o], zpeer[o])
        wait_for(zr_scale.at[o], z_send.at[1, o], z_recv.at[1, o], zpeer[o])
        total = total + decode(zr[o], zr_scale[o])
    sel = -(total * mask)
    for s in range(SNODES):
        sel_ref[s] = sel[s * wide : (s + 1) * wide]

    code, scale = encode(sel)
    ts[...] = code
    ts_scale[...] = scale
    hand_over(ts, tr, t_sem.at[0], tr)
    hand_over(ts_scale, tr_scale, t_sem.at[1], tr_scale)
    moved = decode(tr[...], tr_scale[...])
    high = moved.astype(BF16)
    low = (moved - high.astype(F32)).astype(BF16)
    for s in range(SNODES):
        part = slice(s * wide, (s + 1) * wide)
        term = lax.dot_general(high[part], sorted_panel[s], NT, preferred_element_type=F32) + lax.dot_general(
            low[part], sorted_panel[s], NT, preferred_element_type=F32
        )
        for i in range(wide // 8):
            for k in range(tiles_across):
                dpart[(s * (wide // 8) + i) * tiles_across + k] = term[i * 8 : i * 8 + 8, k * 128 : k * 128 + 128]

    number = q + nq * core

    def scatter(j, carry):
        c, cc = lax.rem(j, nq), j // nq
        there = (row_of(c // 2 + mine // 2, (c + mine) % 2, cc), c)
        same = jnp.logical_and(there[0] == prow, there[1] == q)

        @pl.when(same)
        def _():
            pltpu.make_async_copy(dpart.at[j], dsum_in.at[number], rs_recv.at[number]).start()

        @pl.when(jnp.logical_not(same))
        def _():
            pltpu.make_async_remote_copy(
                src_ref=dpart.at[j], dst_ref=dsum_in.at[number], send_sem=rs_send.at[j],
                recv_sem=rs_recv.at[number], device_id=there, device_id_type=MESH,
            ).start()

        return carry

    lax.fori_loop(0, tiles, scatter, 0)

    @pl.when(number < tiles)
    def _():
        def take(k, carry):
            pltpu.make_async_copy(dsum_in.at[k], dsum_in.at[k], rs_recv.at[k]).wait()
            return carry

        lax.fori_loop(0, 2 * nq, take, 0)
        dtile[...] = jnp.sum(dsum_in[...], axis=0)

        def give(i, carry):
            same = jnp.logical_and(i == prow, mine == q)

            @pl.when(same)
            def _():
                pltpu.make_async_copy(dtile, dfin.at[number], ag_recv.at[number]).start()

            @pl.when(jnp.logical_not(same))
            def _():
                pltpu.make_async_remote_copy(
                    src_ref=dtile, dst_ref=dfin.at[number], send_sem=ag_send.at[i],
                    recv_sem=ag_recv.at[number], device_id=(i, mine), device_id_type=MESH,
                ).start()

            return carry

        lax.fori_loop(0, rows_n, give, 0)

    def collect(j, carry):
        pltpu.make_async_copy(dfin.at[j], dfin.at[j], ag_recv.at[j]).wait()
        return carry

    lax.fori_loop(0, tiles, collect, 0)
    for s in range(SNODES):
        for i in range(wide // 8):
            for k in range(tiles_across):
                here = (s, slice(i * 8, i * 8 + 8), slice(k * 128, k * 128 + 128))
                diag_ref[here] = dinv_ref[here] - dfin[(s * (wide // 8) + i) * tiles_across + k]

    for copy in started:
        copy.wait_send()

    def scatter_done(j, carry):
        c, cc = lax.rem(j, nq), j // nq
        there = (row_of(c // 2 + mine // 2, (c + mine) % 2, cc), c)

        @pl.when(jnp.logical_not(jnp.logical_and(there[0] == prow, there[1] == q)))
        def _():
            pltpu.make_async_copy(dpart.at[j], dpart.at[j], rs_send.at[j]).wait()

        return carry

    lax.fori_loop(0, tiles, scatter_done, 0)

    @pl.when(number < tiles)
    def _():
        def give_done(i, carry):
            @pl.when(jnp.logical_not(jnp.logical_and(i == prow, mine == q)))
            def _():
                pltpu.make_async_copy(dtile, dtile, ag_send.at[i]).wait()

            return carry

        lax.fori_loop(0, rows_n, give_done, 0)


def body(rows_n, cols_n, inverse_blocks, lower_panel, diag_inverse, structure):
    panel_t = jnp.swapaxes(lower_panel, 1, 2)
    dinv_t = jnp.swapaxes(diag_inverse, 1, 2)
    snodes, wide, rows = panel_t.shape
    vb = snodes * wide
    order = dinv_t.shape[2]
    zh_n = cols_n // X
    half = rows_n // 8
    tiles = (vb // 8) * (order // 128)
    vmem = pl.BlockSpec(memory_space=pltpu.VMEM)
    dma = pltpu.SemaphoreType.DMA
    sib_n = 1 + 2 * (half - 1) + 1
    sel_t, diag_t = pl.pallas_call(
        functools.partial(kernel, rows_n, cols_n),
        out_shape=(
            jax.ShapeDtypeStruct((snodes, wide, rows), F32),
            jax.ShapeDtypeStruct((snodes, wide, order), F32),
        ),
        in_specs=[pl.BlockSpec(memory_space=pl.ANY), vmem, vmem, vmem],
        out_specs=(vmem, vmem),
        scratch_shapes=[
            pltpu.VMEM(inverse_blocks.shape, BF16),
            pltpu.VMEM((vb, rows), BF16),
            pltpu.VMEM((2, cols_n * vb, rows), BF16),
            pltpu.VMEM((zh_n, X * vb, rows), F32),
            pltpu.VMEM((zh_n, X - 1, vb, rows), I16),
            pltpu.VMEM((zh_n, X - 1, 1, rows), F32),
            pltpu.VMEM((zh_n, X - 1, vb, rows), I16),
            pltpu.VMEM((zh_n, X - 1, 1, rows), F32),
            pltpu.VMEM((zh_n, vb, rows), F32),
            pltpu.VMEM((zh_n - 1, vb, rows), I16),
            pltpu.VMEM((zh_n - 1, 1, rows), F32),
            pltpu.VMEM((zh_n - 1, vb, rows), I16),
            pltpu.VMEM((zh_n - 1, 1, rows), F32),
            pltpu.VMEM((vb, rows), I16),
            pltpu.VMEM((1, rows), F32),
            pltpu.VMEM((vb, rows), I16),
            pltpu.VMEM((1, rows), F32),
            pltpu.VMEM((snodes, order, rows), BF16),
            pltpu.VMEM((tiles, 8, 128), F32),
            pltpu.VMEM((2 * cols_n, 8, 128), F32),
            pltpu.VMEM((8, 128), F32),
            pltpu.VMEM((tiles, 8, 128), F32),
            dma,
            dma((3,)),
            dma((2,)),
            dma((sib_n,)),
            dma((sib_n,)),
            dma((2, half)),
            dma((2, half)),
            dma((2, zh_n, X - 1)),
            dma((2, zh_n, X - 1)),
            dma((2, zh_n - 1)),
            dma((2, zh_n - 1)),
            dma((2, 3)),
            dma((tiles,)),
            dma((2 * cols_n,)),
            dma((rows_n,)),
            dma((tiles,)),
        ],
        compiler_params=pltpu.CompilerParams(
            collective_id=0, has_side_effects=True, vmem_limit_bytes=40 * 1024 * 1024
        ),
    )(inverse_blocks, panel_t, dinv_t, structure)
    return jnp.swapaxes(sel_t, 1, 2), jnp.swapaxes(diag_t, 1, 2)


def solution(mesh):
    in_specs = (P("prow", "pcol"), P(None, "prow", "pcol"), P(None, None, "pcol"), P())
    out_specs = (P(None, "prow", "pcol"), P(None, None, "pcol"))
    step = functools.partial(body, mesh.shape["prow"], mesh.shape["pcol"])
    return jax.shard_map(step, mesh=mesh, in_specs=in_specs, out_specs=out_specs, check_vma=False)
```

```python
import functools

import jax
import jax.numpy as jnp
from jax import lax
from jax.experimental import pallas as pl
from jax.experimental.pallas import tpu as pltpu
from jax.sharding import PartitionSpec as P

MESH = pl.DeviceIdType.MESH
F32, BF16, I16, I32 = jnp.float32, jnp.bfloat16, jnp.int16, jnp.int32
SNODES = 2
X = 4
NT = (((1,), (1,)), ((), ()))
TINY = 1e-33


def encode(value):
    top = jnp.maximum(jnp.max(jnp.abs(value), axis=0, keepdims=True), TINY)
    code = jnp.round(value * (32767.0 / top)).astype(I32).astype(I16)
    return code, top * (1.0 / 32767.0)


def decode(code, scale):
    return code.astype(I32).astype(F32) * scale


def kernel(
    rows_n, cols_n, a_hbm, l_ref, struct_ref, sel_ref, diag_ref,
    a_ref, panel, local, prod, xs, xs_scale, xr, xr_scale, acc, zs, zs_scale, zr, zr_scale,
    sorted_panel, dpart, dsum_in, dtile, dfin,
    load_sem, h_send, h_recv, y_send, y_recv, zl_send, zl_recv, sib_send, sib_recv, lz_send, lz_recv, lx_send, lx_recv,
    x_send, x_recv, z_send, z_recv, rs_send, rs_recv, ag_send, ag_recv,
):
    wide = l_ref.shape[1]
    rows = l_ref.shape[2]
    vb = SNODES * wide
    nq = cols_n
    y_n = rows_n // 4
    zh_n = nq // X
    tiles_across = nq * wide // 128
    tiles = (vb // 8) * tiles_across
    offsets = [0, -1, 1, -2, 2, -3, 3, 4]
    number_of = {offset: n for n, offset in enumerate(offsets)}

    prow, q = lax.axis_index("prow"), lax.axis_index("pcol")
    p, core = prow // 2, prow % 2
    y, zl = p // 2, p % 2
    zh, x = q // X, q % X
    depth = lax.rem(y - q // 2 + y_n, y_n)
    parity = (zl + q) % 2
    mine = 2 * depth + parity

    def row_of(yy, zz, cc):
        return lax.rem(yy + y_n, y_n) * 4 + zz * 2 + cc

    partner = (row_of(p // 2 + q // 2, (p + q) % 2, core), p)
    source = (q * 2 + core, mine)
    is_self = jnp.logical_and(partner[0] == prow, partner[1] == q)
    away = {o: (row_of(y + o, zl, core), q) for o in (1, -1, 2, -2)}
    across = (row_of(y, 1 - zl, core), q)
    sibling = (row_of(y, zl, 1 - core), q)
    xpeer = [(prow, zh * X + lax.rem(x + o, X)) for o in range(1, X)]
    zpeer = [(prow, lax.rem(zh + o, zh_n) * X + x) for o in range(1, zh_n)]

    barrier = pltpu.get_barrier_semaphore()
    fixed = [*away.values(), across, sibling] + xpeer + zpeer
    for device in fixed:
        pl.semaphore_signal(barrier, inc=1, device_id=device, device_id_type=MESH)

    @pl.when(jnp.logical_not(is_self))
    def _():
        pl.semaphore_signal(barrier, inc=1, device_id=partner, device_id_type=MESH)
        pl.semaphore_signal(barrier, inc=1, device_id=source, device_id_type=MESH)

    load_a = pltpu.make_async_copy(a_hbm, a_ref, load_sem)
    load_a.start()

    lane = lax.broadcasted_iota(I32, (1, rows), 1)
    table = struct_ref[...]
    marks = []
    for s in range(SNODES):
        hits = [
            jnp.max((table[s : s + 1, :] == prow * 2 + b).astype(F32), axis=1, keepdims=True) for b in range(2)
        ]
        marks.append(jnp.where(lane < rows // 2, hits[0], hits[1]))
    mask = jnp.concatenate([jnp.broadcast_to(m, (wide, rows)) for m in marks], axis=0)
    raw = jnp.concatenate([l_ref[s].astype(F32) for s in range(SNODES)], axis=0)
    own = local.at[pl.ds(pl.multiple_of(q * vb, 16), vb), :]
    own[...] = (raw * mask).astype(BF16)

    @pl.when(is_self)
    def _():
        pl.semaphore_wait(barrier, len(fixed))

    @pl.when(jnp.logical_not(is_self))
    def _():
        pl.semaphore_wait(barrier, len(fixed) + 2)

    started = []

    def send(src, dst, send_sem, recv_sem, device):
        copy = pltpu.make_async_remote_copy(
            src_ref=src, dst_ref=dst, send_sem=send_sem, recv_sem=recv_sem, device_id=device, device_id_type=MESH
        )
        copy.start()
        started.append(copy)

    def wait_for(dst, sem):
        pltpu.make_async_copy(dst, dst, sem).wait()

    def block(which, offset, side=0):
        index = lax.rem(depth + offset + y_n, y_n) * 2 + (parity if side == 0 else 1 - parity)
        return panel.at[which, pl.ds(pl.multiple_of(index * vb, 16), vb), :]

    def slot(index):
        return panel.at[core, pl.ds(pl.multiple_of(index * vb, 16), vb), :]

    def piece(index):
        return local.at[pl.ds(pl.multiple_of(index * vb, 16), vb), :]

    @pl.when(is_self)
    def _():
        pltpu.make_async_copy(own, slot(q), h_recv).start()

    @pl.when(jnp.logical_not(is_self))
    def _():
        pltpu.make_async_remote_copy(
            src_ref=own, dst_ref=slot(q), send_sem=h_send, recv_sem=h_recv, device_id=partner, device_id_type=MESH
        ).start()

    def start_local():
        for o in range(1, zh_n):
            send(own, own, lz_send.at[o - 1], lz_recv.at[o - 1], zpeer[o - 1])
        for o in range(1, X):
            send(own, own, lx_send.at[0, o - 1], lx_recv.at[0, o - 1], xpeer[o - 1])

    def pass_local(o):
        there = piece(lax.rem(zh - o + zh_n, zh_n) * X + x)
        wait_for(there, lz_recv.at[o - 1])
        for i in range(1, X):
            send(there, there, lx_send.at[o, i - 1], lx_recv.at[o, i - 1], xpeer[i - 1])

    start_local()
    wait_for(slot(mine), h_recv)

    def along_y(offset, arrives, device):
        src = block(core, offset)
        send(src, src, y_send.at[number_of[arrives]], y_recv.at[number_of[arrives]], device)

    def to_sibling(offset, side):
        n = number_of[offset]
        src = block(core, offset, side)
        send(src, src, sib_send.at[side, n], sib_recv.at[side, n], sibling)

    def spread(offset):
        n = number_of[offset]
        src = block(core, offset)
        send(src, src, zl_send.at[n], zl_recv.at[n], across)
        to_sibling(offset, 0)

    def take_y(offset):
        wait_for(block(core, offset), y_recv.at[number_of[offset]])

    def take_pair(offset):
        wait_for(block(core, offset, 1), zl_recv.at[number_of[offset]])
        to_sibling(offset, 1)

    along_y(0, -2, away[2])
    along_y(0, 2, away[-2])
    along_y(0, -1, away[1])
    along_y(0, 1, away[-1])
    spread(0)

    def multiply(offset):
        n = number_of[offset]
        for side in range(2):
            wait_for(block(1 - core, offset, side), sib_recv.at[side, n])
        b = lax.rem(depth + offset + y_n, y_n)
        group = pl.ds(pl.multiple_of(b * 2 * vb, 16), 2 * vb)
        prod[n] = lax.dot_general(
            panel[0, group, :], a_ref[:, :rows], NT, preferred_element_type=F32
        ) + lax.dot_general(panel[1, group, :], a_ref[:, rows:], NT, preferred_element_type=F32)
        for i in range(2):
            to = 2 * (b % 2) + i
            o = lax.rem(to - x + X, X)

            @pl.when(o == 0)
            def _():
                acc[b // 2] = prod[n, i * vb : (i + 1) * vb, :]

            @pl.when(o > 0)
            def _():
                code, scale = encode(prod[n, i * vb : (i + 1) * vb, :])
                xs[n, i] = code
                xs_scale[n, i] = scale
                for k, (src, dst) in enumerate(((xs, xr), (xs_scale, xr_scale))):
                    pltpu.make_async_remote_copy(
                        src_ref=src.at[n, i], dst_ref=dst.at[b // 2, o - 1], send_sem=x_send.at[k, n, i],
                        recv_sem=x_recv.at[k, b // 2, o - 1], device_id=(prow, zh * X + to), device_id_type=MESH,
                    ).start()

    high_x = x // 2
    odd = (depth + high_x) % 2
    sign = 1 - 2 * high_x

    def reduce_x(r):
        even_way, odd_way = ((0, -1), (-2, 1), (2, -3), (4, 3))[r - 1]
        b = lax.rem(depth + sign * ((1 - odd) * even_way + odd * odd_way) + y_n, y_n)
        g = b // 2
        total = acc[g]
        for o in range(X - 1):
            wait_for(xr.at[g, o], x_recv.at[0, g, o])
            wait_for(xr_scale.at[g, o], x_recv.at[1, g, o])
            total = total + decode(xr[g, o], xr_scale[g, o])
        o = lax.rem(g - zh + zh_n, zh_n)
        acc[g] = total

        @pl.when(o > 0)
        def _():
            code, scale = encode(acc[g])
            zs[o - 1] = code
            zs_scale[o - 1] = scale
            for k, (src, dst) in enumerate(((zs, zr), (zs_scale, zr_scale))):
                pltpu.make_async_remote_copy(
                    src_ref=src.at[o - 1], dst_ref=dst.at[o - 1], send_sem=z_send.at[k, o - 1],
                    recv_sem=z_recv.at[k, o - 1], device_id=(prow, g * X + x), device_id_type=MESH,
                ).start()

    take_pair(0)
    for offset in (-1, 1):
        take_y(offset)
        spread(offset)
    for offset in (-2, 2):
        take_y(offset)
        along_y(offset, 3 if offset > 0 else -3, away[-offset // 2])
    far = 1 - 2 * core
    index = lax.rem(depth - 2 * far + y_n, y_n) * 2 + parity
    across_ring = panel.at[core, pl.ds(pl.multiple_of(index * vb, 16), vb), :]
    send(across_ring, across_ring, y_send.at[7], y_recv.at[7], (row_of(y + 2 * far, zl, core), q))
    for offset in (-2, 2):
        spread(offset)
    for o in range(1, zh_n):
        pass_local(o)
    load_a.wait()
    multiply(0)
    for offset in (-1, 1):
        take_pair(offset)
        multiply(offset)
    for offset in (-3, 3, 4):
        take_y(offset)
        spread(offset)
    for r in (2, 3):
        for offset in (-r, r):
            take_pair(offset)
            multiply(offset)
    reduce_x(1)
    take_pair(4)
    multiply(4)
    reduce_x(2)
    reduce_x(3)

    for o in range(zh_n):
        for i in range(1, X):
            wait_for(
                piece(lax.rem(zh - o + zh_n, zh_n) * X + lax.rem(x - i + X, X)), lx_recv.at[o, i - 1]
            )
    for s in range(SNODES):
        for k in range(0, nq, 2):
            pieces = [local[(k + i) * vb : (k + i + 1) * vb, :].astype(F32) for i in range(2)]
            both = jnp.concatenate([part[s * wide : (s + 1) * wide] for part in pieces], axis=0)
            sorted_panel[s, k * wide : (k + 2) * wide, :] = both.astype(BF16)

    reduce_x(4)
    total = acc[zh]
    for o in range(zh_n - 1):
        wait_for(zr.at[o], z_recv.at[0, o])
        wait_for(zr_scale.at[o], z_recv.at[1, o])
        total = total + decode(zr[o], zr_scale[o])
    sel = -(total * mask)
    for s in range(SNODES):
        sel_ref[s] = sel[s * wide : (s + 1) * wide]

    high = sel.astype(BF16)
    low = (sel - high.astype(F32)).astype(BF16)
    for s in range(SNODES):
        part = slice(s * wide, (s + 1) * wide)
        term = lax.dot_general(high[part], sorted_panel[s], NT, preferred_element_type=F32) + lax.dot_general(
            low[part], sorted_panel[s], NT, preferred_element_type=F32
        )
        for i in range(wide // 8):
            for k in range(tiles_across):
                dpart[(s * (wide // 8) + i) * tiles_across + k] = term[i * 8 : i * 8 + 8, k * 128 : k * 128 + 128]

    chips = rows_n // 2
    number = p + chips * core

    def handler(j):
        return lax.rem(j, chips) * 2 + j // chips

    def scatter(j, carry):
        there = handler(j)

        @pl.when(there == prow)
        def _():
            pltpu.make_async_copy(dpart.at[j], dsum_in.at[prow], rs_recv.at[prow]).start()

        @pl.when(there != prow)
        def _():
            pltpu.make_async_remote_copy(
                src_ref=dpart.at[j], dst_ref=dsum_in.at[prow], send_sem=rs_send.at[j],
                recv_sem=rs_recv.at[prow], device_id=(there, q), device_id_type=MESH,
            ).start()

        return carry

    lax.fori_loop(0, tiles, scatter, 0)

    @pl.when(number < tiles)
    def _():
        def take(k, carry):
            wait_for(dsum_in.at[k], rs_recv.at[k])
            return carry

        lax.fori_loop(0, rows_n, take, 0)
        dtile[...] = jnp.sum(dsum_in[...], axis=0)

        def give(i, carry):
            @pl.when(i == prow)
            def _():
                pltpu.make_async_copy(dtile, dfin.at[number], ag_recv.at[number]).start()

            @pl.when(i != prow)
            def _():
                pltpu.make_async_remote_copy(
                    src_ref=dtile, dst_ref=dfin.at[number], send_sem=ag_send.at[i],
                    recv_sem=ag_recv.at[number], device_id=(i, q), device_id_type=MESH,
                ).start()

            return carry

        lax.fori_loop(0, rows_n, give, 0)

    def collect(j, carry):
        wait_for(dfin.at[j], ag_recv.at[j])
        return carry

    lax.fori_loop(0, tiles, collect, 0)
    for s in range(SNODES):
        for i in range(wide // 8):
            for k in range(tiles_across):
                here = (s, slice(i * 8, i * 8 + 8), slice(k * 128, k * 128 + 128))
                diag_ref[here] = dfin[(s * (wide // 8) + i) * tiles_across + k]

    for copy in started:
        copy.wait_send()

    @pl.when(jnp.logical_not(is_self))
    def _():
        wait_for(own, h_send)

    for offset in offsets:
        n = number_of[offset]
        b = lax.rem(depth + offset + y_n, y_n)
        for i in range(2):
            @pl.when(2 * (b % 2) + i != x)
            def _():
                wait_for(xs.at[n, i], x_send.at[0, n, i])
                wait_for(xs_scale.at[n, i], x_send.at[1, n, i])

    for o in range(zh_n - 1):
        wait_for(zs.at[o], z_send.at[0, o])
        wait_for(zs_scale.at[o], z_send.at[1, o])

    def scatter_done(j, carry):
        @pl.when(handler(j) != prow)
        def _():
            wait_for(dpart.at[j], rs_send.at[j])

        return carry

    lax.fori_loop(0, tiles, scatter_done, 0)

    @pl.when(number < tiles)
    def _():
        def give_done(i, carry):
            @pl.when(i != prow)
            def _():
                wait_for(dtile, ag_send.at[i])

            return carry

        lax.fori_loop(0, rows_n, give_done, 0)


def body(rows_n, cols_n, inverse_blocks, lower_panel, diag_inverse, structure):
    panel_t = jnp.swapaxes(lower_panel, 1, 2)
    snodes, wide, rows = panel_t.shape
    vb = snodes * wide
    order = diag_inverse.shape[1]
    zh_n = cols_n // X
    y_n = rows_n // 4
    tiles = (vb // 8) * (order // 128)
    vmem = pl.BlockSpec(memory_space=pltpu.VMEM)
    dma = pltpu.SemaphoreType.DMA
    hbm = pl.BlockSpec(memory_space=pltpu.HBM)
    sel_t, diag_t = pl.pallas_call(
        functools.partial(kernel, rows_n, cols_n),
        out_shape=(
            jax.ShapeDtypeStruct((snodes, wide, rows), F32),
            jax.ShapeDtypeStruct((snodes, wide, order), F32),
        ),
        in_specs=[hbm, vmem, vmem],
        out_specs=(vmem, vmem),
        scratch_shapes=[
            pltpu.VMEM(inverse_blocks.shape, BF16),
            pltpu.VMEM((2, cols_n * vb, rows), BF16),
            pltpu.VMEM((cols_n * vb, rows), BF16),
            pltpu.VMEM((y_n, 2 * vb, rows), F32),
            pltpu.VMEM((y_n, 2, vb, rows), I16),
            pltpu.VMEM((y_n, 2, 1, rows), F32),
            pltpu.VMEM((zh_n, X - 1, vb, rows), I16),
            pltpu.VMEM((zh_n, X - 1, 1, rows), F32),
            pltpu.VMEM((zh_n, vb, rows), F32),
            pltpu.VMEM((zh_n - 1, vb, rows), I16),
            pltpu.VMEM((zh_n - 1, 1, rows), F32),
            pltpu.VMEM((zh_n - 1, vb, rows), I16),
            pltpu.VMEM((zh_n - 1, 1, rows), F32),
            pltpu.VMEM((snodes, order, rows), BF16),
            pltpu.VMEM((tiles, 8, 128), F32),
            pltpu.VMEM((rows_n, 8, 128), F32),
            pltpu.VMEM((8, 128), F32),
            pltpu.VMEM((tiles, 8, 128), F32),
            dma,
            dma,
            dma,
            dma((y_n,)),
            dma((y_n,)),
            dma((y_n,)),
            dma((y_n,)),
            dma((2, y_n)),
            dma((2, y_n)),
            dma((zh_n - 1,)),
            dma((zh_n - 1,)),
            dma((zh_n, X - 1)),
            dma((zh_n, X - 1)),
            dma((2, y_n, 2)),
            dma((2, zh_n, X - 1)),
            dma((2, zh_n - 1)),
            dma((2, zh_n - 1)),
            dma((tiles,)),
            dma((rows_n,)),
            dma((rows_n,)),
            dma((tiles,)),
        ],
        compiler_params=pltpu.CompilerParams(
            collective_id=0, has_side_effects=True, vmem_limit_bytes=53 * 1024 * 1024
        ),
    )(inverse_blocks, panel_t, structure)
    return jnp.swapaxes(sel_t, 1, 2), diag_inverse - jnp.swapaxes(diag_t, 1, 2)


def solution(mesh):
    in_specs = (P("prow", "pcol"), P(None, "prow", "pcol"), P(None, None, "pcol"), P())
    out_specs = (P(None, "prow", "pcol"), P(None, None, "pcol"))
    step = functools.partial(body, mesh.shape["prow"], mesh.shape["pcol"])
    return jax.shard_map(step, mesh=mesh, in_specs=in_specs, out_specs=out_specs, check_vma=False)
```

```python
import functools

import jax
import jax.numpy as jnp
from jax import lax
from jax.experimental import pallas as pl
from jax.experimental.pallas import tpu as pltpu
from jax.sharding import PartitionSpec as P

MESH = pl.DeviceIdType.MESH
F32, BF16, I16, I32 = jnp.float32, jnp.bfloat16, jnp.int16, jnp.int32
SNODES = 2
X = 4
NT = (((1,), (1,)), ((), ()))
TINY = 1e-33


def encode(value):
    top = jnp.maximum(jnp.max(jnp.abs(value), axis=0, keepdims=True), TINY)
    code = jnp.round(value * (32767.0 / top)).astype(I32).astype(I16)
    return code, top * (1.0 / 32767.0)


def decode(code, scale):
    return code.astype(I32).astype(F32) * scale


def kernel(
    rows_n, cols_n, a_hbm, l_ref, struct_ref, sel_ref, diag_ref,
    a_ref, panel, local, prod, xs, xs_scale, xr, xr_scale, acc, zs, zs_scale, zr, zr_scale,
    sorted_panel, dpart, dsum_in, dtile, dfin,
    load_sem, h_send, h_recv, y_send, y_recv, zl_send, zl_recv, sib_send, sib_recv, lz_send, lz_recv, lx_send, lx_recv,
    x_send, x_recv, z_send, z_recv, rs_send, rs_recv, ag_send, ag_recv,
):
    wide = l_ref.shape[1]
    rows = l_ref.shape[2]
    vb = SNODES * wide
    nq = cols_n
    y_n = rows_n // 4
    zh_n = nq // X
    tiles_across = nq * wide // 128
    tiles = (vb // 8) * tiles_across
    offsets = [0, -1, 1, -2, 2, -3, 3, 4]
    number_of = {offset: n for n, offset in enumerate(offsets)}

    prow, q = lax.axis_index("prow"), lax.axis_index("pcol")
    p, core = prow // 2, prow % 2
    y, zl = p // 2, p % 2
    zh, x = q // X, q % X
    depth = lax.rem(y - q // 2 + y_n, y_n)
    parity = (zl + q) % 2
    mine = 2 * depth + parity

    def row_of(yy, zz, cc):
        return lax.rem(yy + y_n, y_n) * 4 + zz * 2 + cc

    shift = 2 * lax.rem(p // X - zh + zh_n + zh_n // 2, zh_n) + x // 2
    partner = (row_of(p // 2 + shift, (p + x) % 2, core), p)

    def z_of(index):
        return lax.rem(zh + zh_n // 2 - index // 2 + zh_n, zh_n)

    source = (q * 2 + core, z_of(depth) * X + 2 * (depth % 2) + parity)
    is_self = jnp.logical_and(partner[0] == prow, partner[1] == q)
    away = {o: (row_of(y + o, zl, core), q) for o in (1, -1, 2, -2)}
    across = (row_of(y, 1 - zl, core), q)
    sibling = (row_of(y, zl, 1 - core), q)
    xpeer = [(prow, zh * X + lax.rem(x + o, X)) for o in range(1, X)]
    zpeer = [(prow, lax.rem(zh + o, zh_n) * X + x) for o in range(1, zh_n)]

    barrier = pltpu.get_barrier_semaphore()
    @pl.when(jnp.logical_not(is_self))
    def _():
        pl.semaphore_signal(barrier, inc=1, device_id=partner, device_id_type=MESH)
        pl.semaphore_signal(barrier, inc=1, device_id=source, device_id_type=MESH)

    fixed = [*away.values(), across, sibling] + xpeer + zpeer
    for device in fixed:
        pl.semaphore_signal(barrier, inc=1, device_id=device, device_id_type=MESH)

    load_a = pltpu.make_async_copy(a_hbm, a_ref, load_sem)
    load_a.start()

    lane = lax.broadcasted_iota(I32, (1, rows), 1)
    table = struct_ref[...]
    marks = []
    for s in range(SNODES):
        hits = [
            jnp.max((table[s : s + 1, :] == prow * 2 + b).astype(F32), axis=1, keepdims=True) for b in range(2)
        ]
        marks.append(jnp.where(lane < rows // 2, hits[0], hits[1]))
    mask = jnp.concatenate([jnp.broadcast_to(m, (wide, rows)) for m in marks], axis=0)
    raw = jnp.concatenate([l_ref[s].astype(F32) for s in range(SNODES)], axis=0)
    own = local.at[pl.ds(pl.multiple_of(q * vb, 16), vb), :]
    own[...] = (raw * mask).astype(BF16)

    @pl.when(is_self)
    def _():
        pl.semaphore_wait(barrier, len(fixed))

    @pl.when(jnp.logical_not(is_self))
    def _():
        pl.semaphore_wait(barrier, len(fixed) + 2)

    started = []

    def send(src, dst, send_sem, recv_sem, device):
        copy = pltpu.make_async_remote_copy(
            src_ref=src, dst_ref=dst, send_sem=send_sem, recv_sem=recv_sem, device_id=device, device_id_type=MESH
        )
        copy.start()
        started.append(copy)

    def wait_for(dst, sem):
        pltpu.make_async_copy(dst, dst, sem).wait()

    def block(which, offset, side=0):
        index = lax.rem(depth + offset + y_n, y_n) * 2 + (parity if side == 0 else 1 - parity)
        return panel.at[which, pl.ds(pl.multiple_of(index * vb, 16), vb), :]

    def slot(index):
        return panel.at[core, pl.ds(pl.multiple_of(index * vb, 16), vb), :]

    def piece(index):
        return local.at[pl.ds(pl.multiple_of(index * vb, 16), vb), :]

    @pl.when(is_self)
    def _():
        pltpu.make_async_copy(own, slot(2 * shift + x % 2), h_recv).start()

    @pl.when(jnp.logical_not(is_self))
    def _():
        pltpu.make_async_remote_copy(
            src_ref=own, dst_ref=slot(2 * shift + x % 2), send_sem=h_send, recv_sem=h_recv, device_id=partner, device_id_type=MESH
        ).start()

    def start_local():
        for o in range(1, zh_n):
            send(own, own, lz_send.at[o - 1], lz_recv.at[o - 1], zpeer[o - 1])
        for o in range(1, X):
            send(own, own, lx_send.at[0, o - 1], lx_recv.at[0, o - 1], xpeer[o - 1])

    def pass_local(o):
        there = piece(lax.rem(zh - o + zh_n, zh_n) * X + x)
        wait_for(there, lz_recv.at[o - 1])
        for i in range(1, X):
            send(there, there, lx_send.at[o, i - 1], lx_recv.at[o, i - 1], xpeer[i - 1])

    start_local()
    wait_for(slot(mine), h_recv)

    def along_y(offset, arrives, device):
        src = block(core, offset)
        send(src, src, y_send.at[number_of[arrives]], y_recv.at[number_of[arrives]], device)

    def to_sibling(offset, side):
        n = number_of[offset]
        src = block(core, offset, side)
        send(src, src, sib_send.at[side, n], sib_recv.at[side, n], sibling)

    def spread(offset):
        n = number_of[offset]
        src = block(core, offset)
        send(src, src, zl_send.at[n], zl_recv.at[n], across)
        to_sibling(offset, 0)

    def take_y(offset):
        wait_for(block(core, offset), y_recv.at[number_of[offset]])

    def take_pair(offset):
        wait_for(block(core, offset, 1), zl_recv.at[number_of[offset]])
        to_sibling(offset, 1)

    along_y(0, -2, away[2])
    along_y(0, 2, away[-2])
    along_y(0, -1, away[1])
    along_y(0, 1, away[-1])
    spread(0)

    def multiply(offset):
        n = number_of[offset]
        for side in range(2):
            wait_for(block(1 - core, offset, side), sib_recv.at[side, n])
        b = lax.rem(depth + offset + y_n, y_n)
        group = pl.ds(pl.multiple_of(b * 2 * vb, 16), 2 * vb)
        prod[n] = lax.dot_general(
            panel[0, group, :], a_ref[:, :rows], NT, preferred_element_type=F32
        ) + lax.dot_general(panel[1, group, :], a_ref[:, rows:], NT, preferred_element_type=F32)
        for i in range(2):
            to = 2 * (b % 2) + i
            o = lax.rem(to - x + X, X)

            @pl.when(o == 0)
            def _():
                acc[z_of(b)] = prod[n, i * vb : (i + 1) * vb, :]

            @pl.when(o > 0)
            def _():
                code, scale = encode(prod[n, i * vb : (i + 1) * vb, :])
                xs[n, i] = code
                xs_scale[n, i] = scale
                for k, (src, dst) in ((1, (xs_scale, xr_scale)), (0, (xs, xr))):
                    pltpu.make_async_remote_copy(
                        src_ref=src.at[n, i], dst_ref=dst.at[z_of(b), o - 1], send_sem=x_send.at[k, n, i],
                        recv_sem=x_recv.at[k, z_of(b), o - 1], device_id=(prow, zh * X + to), device_id_type=MESH,
                    ).start()

    high_x = x // 2
    odd = (depth + high_x) % 2
    sign = 1 - 2 * high_x

    def reduce_x(r):
        even_way, odd_way = ((0, -1), (-2, 1), (2, -3), (4, 3))[r - 1]
        b = lax.rem(depth + sign * ((1 - odd) * even_way + odd * odd_way) + y_n, y_n)
        g = z_of(b)
        total = acc[g]
        for o in range(X - 1):
            wait_for(xr.at[g, o], x_recv.at[0, g, o])
            wait_for(xr_scale.at[g, o], x_recv.at[1, g, o])
            total = total + decode(xr[g, o], xr_scale[g, o])
        o = lax.rem(g - zh + zh_n, zh_n)
        acc[g] = total

        @pl.when(o > 0)
        def _():
            code, scale = encode(acc[g])
            zs[o - 1] = code
            zs_scale[o - 1] = scale
            for k, (src, dst) in ((1, (zs_scale, zr_scale)), (0, (zs, zr))):
                pltpu.make_async_remote_copy(
                    src_ref=src.at[o - 1], dst_ref=dst.at[o - 1], send_sem=z_send.at[k, o - 1],
                    recv_sem=z_recv.at[k, o - 1], device_id=(prow, g * X + x), device_id_type=MESH,
                ).start()

    take_pair(0)
    for o in range(1, zh_n):
        pass_local(o)
    for offset in (-1, 1):
        take_y(offset)
        spread(offset)
    for offset in (-2, 2):
        take_y(offset)
        along_y(offset, 3 if offset > 0 else -3, away[-offset // 2])
    far = 1 - 2 * core
    index = lax.rem(depth - 2 * far + y_n, y_n) * 2 + parity
    across_ring = panel.at[core, pl.ds(pl.multiple_of(index * vb, 16), vb), :]
    send(across_ring, across_ring, y_send.at[7], y_recv.at[7], (row_of(y + 2 * far, zl, core), q))
    for offset in (-2, 2):
        spread(offset)
    load_a.wait()
    multiply(0)
    for offset in (-1, 1):
        take_pair(offset)
        multiply(offset)
    for offset in (-3, 3, 4):
        take_y(offset)
        spread(offset)
    for r in (2, 3):
        for offset in (-r, r):
            take_pair(offset)
            multiply(offset)
    reduce_x(1)
    take_pair(4)
    multiply(4)
    reduce_x(2)
    reduce_x(3)

    for o in range(zh_n):
        for i in range(1, X):
            wait_for(
                piece(lax.rem(zh - o + zh_n, zh_n) * X + lax.rem(x - i + X, X)), lx_recv.at[o, i - 1]
            )
    for s in range(SNODES):
        for k in range(0, nq, 2):
            pieces = [local[(k + i) * vb : (k + i + 1) * vb, :].astype(F32) for i in range(2)]
            both = jnp.concatenate([part[s * wide : (s + 1) * wide] for part in pieces], axis=0)
            sorted_panel[s, k * wide : (k + 2) * wide, :] = both.astype(BF16)

    reduce_x(4)
    total = acc[zh]
    for o in range(zh_n - 1):
        wait_for(zr.at[o], z_recv.at[0, o])
        wait_for(zr_scale.at[o], z_recv.at[1, o])
        total = total + decode(zr[o], zr_scale[o])
    sel = -(total * mask)
    for s in range(SNODES):
        sel_ref[s] = sel[s * wide : (s + 1) * wide]

    high = sel.astype(BF16)
    low = (sel - high.astype(F32)).astype(BF16)
    for s in range(SNODES):
        part = slice(s * wide, (s + 1) * wide)
        term = lax.dot_general(high[part], sorted_panel[s], NT, preferred_element_type=F32) + lax.dot_general(
            low[part], sorted_panel[s], NT, preferred_element_type=F32
        )
        for i in range(wide // 8):
            for k in range(tiles_across):
                dpart[(s * (wide // 8) + i) * tiles_across + k] = term[i * 8 : i * 8 + 8, k * 128 : k * 128 + 128]

    chips = rows_n // 2
    number = p + chips * core

    def handler(j):
        return lax.rem(j, chips) * 2 + j // chips

    def scatter(j, carry):
        there = handler(j)

        @pl.when(there == prow)
        def _():
            pltpu.make_async_copy(dpart.at[j], dsum_in.at[prow], rs_recv.at[prow]).start()

        @pl.when(there != prow)
        def _():
            pltpu.make_async_remote_copy(
                src_ref=dpart.at[j], dst_ref=dsum_in.at[prow], send_sem=rs_send.at[j],
                recv_sem=rs_recv.at[prow], device_id=(there, q), device_id_type=MESH,
            ).start()

        return carry

    lax.fori_loop(0, tiles, scatter, 0)

    @pl.when(number < tiles)
    def _():
        def take(k, carry):
            wait_for(dsum_in.at[k], rs_recv.at[k])
            return carry

        lax.fori_loop(0, rows_n, take, 0)
        dtile[...] = jnp.sum(dsum_in[...], axis=0)

        def give(i, carry):
            @pl.when(i == prow)
            def _():
                pltpu.make_async_copy(dtile, dfin.at[number], ag_recv.at[number]).start()

            @pl.when(i != prow)
            def _():
                pltpu.make_async_remote_copy(
                    src_ref=dtile, dst_ref=dfin.at[number], send_sem=ag_send.at[i],
                    recv_sem=ag_recv.at[number], device_id=(i, q), device_id_type=MESH,
                ).start()

            return carry

        lax.fori_loop(0, rows_n, give, 0)

    def collect(j, carry):
        wait_for(dfin.at[j], ag_recv.at[j])
        return carry

    lax.fori_loop(0, tiles, collect, 0)
    for s in range(SNODES):
        for i in range(wide // 8):
            for k in range(tiles_across):
                here = (s, slice(i * 8, i * 8 + 8), slice(k * 128, k * 128 + 128))
                diag_ref[here] = dfin[(s * (wide // 8) + i) * tiles_across + k]

    for copy in started:
        copy.wait_send()

    @pl.when(jnp.logical_not(is_self))
    def _():
        wait_for(own, h_send)

    for offset in offsets:
        n = number_of[offset]
        b = lax.rem(depth + offset + y_n, y_n)
        for i in range(2):
            @pl.when(2 * (b % 2) + i != x)
            def _():
                wait_for(xs.at[n, i], x_send.at[0, n, i])
                wait_for(xs_scale.at[n, i], x_send.at[1, n, i])

    for o in range(zh_n - 1):
        wait_for(zs.at[o], z_send.at[0, o])
        wait_for(zs_scale.at[o], z_send.at[1, o])

    def scatter_done(j, carry):
        @pl.when(handler(j) != prow)
        def _():
            wait_for(dpart.at[j], rs_send.at[j])

        return carry

    lax.fori_loop(0, tiles, scatter_done, 0)

    @pl.when(number < tiles)
    def _():
        def give_done(i, carry):
            @pl.when(i != prow)
            def _():
                wait_for(dtile, ag_send.at[i])

            return carry

        lax.fori_loop(0, rows_n, give_done, 0)


def body(rows_n, cols_n, inverse_blocks, lower_panel, diag_inverse, structure):
    panel_t = jnp.swapaxes(lower_panel, 1, 2)
    snodes, wide, rows = panel_t.shape
    vb = snodes * wide
    order = diag_inverse.shape[1]
    zh_n = cols_n // X
    y_n = rows_n // 4
    tiles = (vb // 8) * (order // 128)
    vmem = pl.BlockSpec(memory_space=pltpu.VMEM)
    dma = pltpu.SemaphoreType.DMA
    hbm = pl.BlockSpec(memory_space=pltpu.HBM)
    sel_t, diag_t = pl.pallas_call(
        functools.partial(kernel, rows_n, cols_n),
        out_shape=(
            jax.ShapeDtypeStruct((snodes, wide, rows), F32),
            jax.ShapeDtypeStruct((snodes, wide, order), F32),
        ),
        in_specs=[hbm, vmem, vmem],
        out_specs=(vmem, vmem),
        scratch_shapes=[
            pltpu.VMEM(inverse_blocks.shape, BF16),
            pltpu.VMEM((2, cols_n * vb, rows), BF16),
            pltpu.VMEM((cols_n * vb, rows), BF16),
            pltpu.VMEM((y_n, 2 * vb, rows), F32),
            pltpu.VMEM((y_n, 2, vb, rows), I16),
            pltpu.VMEM((y_n, 2, 1, rows), F32),
            pltpu.VMEM((zh_n, X - 1, vb, rows), I16),
            pltpu.VMEM((zh_n, X - 1, 1, rows), F32),
            pltpu.VMEM((zh_n, vb, rows), F32),
            pltpu.VMEM((zh_n - 1, vb, rows), I16),
            pltpu.VMEM((zh_n - 1, 1, rows), F32),
            pltpu.VMEM((zh_n - 1, vb, rows), I16),
            pltpu.VMEM((zh_n - 1, 1, rows), F32),
            pltpu.VMEM((snodes, order, rows), BF16),
            pltpu.VMEM((tiles, 8, 128), F32),
            pltpu.VMEM((rows_n, 8, 128), F32),
            pltpu.VMEM((8, 128), F32),
            pltpu.VMEM((tiles, 8, 128), F32),
            dma,
            dma,
            dma,
            dma((y_n,)),
            dma((y_n,)),
            dma((y_n,)),
            dma((y_n,)),
            dma((2, y_n)),
            dma((2, y_n)),
            dma((zh_n - 1,)),
            dma((zh_n - 1,)),
            dma((zh_n, X - 1)),
            dma((zh_n, X - 1)),
            dma((2, y_n, 2)),
            dma((2, zh_n, X - 1)),
            dma((2, zh_n - 1)),
            dma((2, zh_n - 1)),
            dma((tiles,)),
            dma((rows_n,)),
            dma((rows_n,)),
            dma((tiles,)),
        ],
        compiler_params=pltpu.CompilerParams(
            collective_id=0, has_side_effects=True, vmem_limit_bytes=53 * 1024 * 1024
        ),
    )(inverse_blocks, panel_t, structure)
    return jnp.swapaxes(sel_t, 1, 2), diag_inverse - jnp.swapaxes(diag_t, 1, 2)


def solution(mesh):
    in_specs = (P("prow", "pcol"), P(None, "prow", "pcol"), P(None, None, "pcol"), P())
    out_specs = (P(None, "prow", "pcol"), P(None, None, "pcol"))
    step = functools.partial(body, mesh.shape["prow"], mesh.shape["pcol"])
    return jax.shard_map(step, mesh=mesh, in_specs=in_specs, out_specs=out_specs, check_vma=False)
```

```python
import functools

import jax
import jax.numpy as jnp
from jax import lax
from jax.experimental import pallas as pl
from jax.experimental.pallas import tpu as pltpu
from jax.sharding import PartitionSpec as P

MESH = pl.DeviceIdType.MESH
F32, BF16, I16, I32 = jnp.float32, jnp.bfloat16, jnp.int16, jnp.int32
SNODES = 2
X = 4
NT = (((1,), (1,)), ((), ()))
TINY = 1e-33


def encode(value):
    top = jnp.maximum(jnp.max(jnp.abs(value), axis=0, keepdims=True), TINY)
    code = jnp.round(value * (32767.0 / top)).astype(I32).astype(I16)
    return code, top * (1.0 / 32767.0)


def decode(code, scale):
    return code.astype(I32).astype(F32) * scale


def kernel(
    rows_n, cols_n, a_hbm, l_ref, struct_ref, sel_ref, diag_ref,
    a_ref, panel, local, prod, xs, xs_scale, xr, xr_scale, acc, zs, zs_scale, zr, zr_scale,
    sorted_panel, dpart, dsum_in, dtile, dfin,
    load_sem, h_send, h_recv, y_send, y_recv, zl_send, zl_recv, sib_send, sib_recv, lz_send, lz_recv, lx_send, lx_recv,
    x_send, x_recv, z_send, z_recv, rs_send, rs_recv, ag_send, ag_recv,
):
    wide = l_ref.shape[1]
    rows = l_ref.shape[2]
    vb = SNODES * wide
    nq = cols_n
    y_n = rows_n // 4
    zh_n = nq // X
    tiles_across = nq * wide // 128
    tiles = (vb // 8) * tiles_across
    offsets = [0, -1, 1, -2, 2, -3, 3, 4]
    number_of = {offset: n for n, offset in enumerate(offsets)}

    prow, q = lax.axis_index("prow"), lax.axis_index("pcol")
    p, core = prow // 2, prow % 2
    y, zl = p // 2, p % 2
    zh, x = q // X, q % X
    depth = lax.rem(y - q // 2 + y_n, y_n)
    parity = (zl + q) % 2
    mine = 2 * depth + parity

    def row_of(yy, zz, cc):
        return lax.rem(yy + y_n, y_n) * 4 + zz * 2 + cc

    shift = 2 * lax.rem(p // X - zh + zh_n + zh_n // 2, zh_n) + x // 2
    partner = (row_of(p // 2 + shift, (p + x) % 2, core), p)

    def z_of(index):
        return lax.rem(zh + zh_n // 2 - index // 2 + zh_n, zh_n)

    source = (q * 2 + core, z_of(depth) * X + 2 * (depth % 2) + parity)
    is_self = jnp.logical_and(partner[0] == prow, partner[1] == q)
    away = {o: (row_of(y + o, zl, core), q) for o in (1, -1, 2, -2)}
    across = (row_of(y, 1 - zl, core), q)
    sibling = (row_of(y, zl, 1 - core), q)
    xpeer = [(prow, zh * X + lax.rem(x + o, X)) for o in range(1, X)]
    zpeer = [(prow, lax.rem(zh + o, zh_n) * X + x) for o in range(1, zh_n)]

    barrier = pltpu.get_barrier_semaphore()
    @pl.when(jnp.logical_not(is_self))
    def _():
        pl.semaphore_signal(barrier, inc=1, device_id=partner, device_id_type=MESH)
        pl.semaphore_signal(barrier, inc=1, device_id=source, device_id_type=MESH)

    fixed = [*away.values(), across, sibling] + xpeer + zpeer
    for device in fixed:
        pl.semaphore_signal(barrier, inc=1, device_id=device, device_id_type=MESH)

    load_a = pltpu.make_async_copy(a_hbm, a_ref, load_sem)
    load_a.start()

    lane = lax.broadcasted_iota(I32, (1, rows), 1)
    table = struct_ref[...]
    marks = []
    for s in range(SNODES):
        hits = [
            jnp.max((table[s : s + 1, :] == prow * 2 + b).astype(F32), axis=1, keepdims=True) for b in range(2)
        ]
        marks.append(jnp.where(lane < rows // 2, hits[0], hits[1]))
    mask = jnp.concatenate([jnp.broadcast_to(m, (wide, rows)) for m in marks], axis=0)
    raw = jnp.concatenate([l_ref[s].astype(F32) for s in range(SNODES)], axis=0)
    own = local.at[pl.ds(pl.multiple_of(q * vb, 16), vb), :]
    own[...] = (raw * mask).astype(BF16)

    @pl.when(is_self)
    def _():
        pl.semaphore_wait(barrier, len(fixed))

    @pl.when(jnp.logical_not(is_self))
    def _():
        pl.semaphore_wait(barrier, len(fixed) + 2)

    started = []

    def send(src, dst, send_sem, recv_sem, device):
        copy = pltpu.make_async_remote_copy(
            src_ref=src, dst_ref=dst, send_sem=send_sem, recv_sem=recv_sem, device_id=device, device_id_type=MESH
        )
        copy.start()
        started.append(copy)

    def wait_for(dst, sem):
        pltpu.make_async_copy(dst, dst, sem).wait()

    def block(which, offset, side=0):
        index = lax.rem(depth + offset + y_n, y_n) * 2 + (parity if side == 0 else 1 - parity)
        return panel.at[which, pl.ds(pl.multiple_of(index * vb, 16), vb), :]

    def slot(index):
        return panel.at[core, pl.ds(pl.multiple_of(index * vb, 16), vb), :]

    def piece(index):
        return local.at[pl.ds(pl.multiple_of(index * vb, 16), vb), :]

    @pl.when(is_self)
    def _():
        pltpu.make_async_copy(own, slot(2 * shift + x % 2), h_recv).start()

    @pl.when(jnp.logical_not(is_self))
    def _():
        pltpu.make_async_remote_copy(
            src_ref=own, dst_ref=slot(2 * shift + x % 2), send_sem=h_send, recv_sem=h_recv, device_id=partner, device_id_type=MESH
        ).start()

    def start_local():
        for o in range(1, zh_n):
            send(own, own, lz_send.at[o - 1], lz_recv.at[o - 1], zpeer[o - 1])
        for o in range(1, X):
            send(own, own, lx_send.at[0, o - 1], lx_recv.at[0, o - 1], xpeer[o - 1])

    def pass_local(o):
        there = piece(lax.rem(zh - o + zh_n, zh_n) * X + x)
        wait_for(there, lz_recv.at[o - 1])
        for i in range(1, X):
            send(there, there, lx_send.at[o, i - 1], lx_recv.at[o, i - 1], xpeer[i - 1])

    start_local()
    wait_for(slot(mine), h_recv)

    def along_y(offset, arrives, device):
        src = block(core, offset)
        send(src, src, y_send.at[number_of[arrives]], y_recv.at[number_of[arrives]], device)

    def to_sibling(offset, side):
        n = number_of[offset]
        src = block(core, offset, side)
        send(src, src, sib_send.at[side, n], sib_recv.at[side, n], sibling)

    def spread(offset):
        n = number_of[offset]
        src = block(core, offset)
        send(src, src, zl_send.at[n], zl_recv.at[n], across)
        to_sibling(offset, 0)

    def take_y(offset):
        wait_for(block(core, offset), y_recv.at[number_of[offset]])

    def take_pair(offset):
        wait_for(block(core, offset, 1), zl_recv.at[number_of[offset]])
        to_sibling(offset, 1)

    along_y(0, -2, away[2])
    along_y(0, 2, away[-2])
    along_y(0, -1, away[1])
    along_y(0, 1, away[-1])
    spread(0)

    def multiply(offset):
        n = number_of[offset]
        for side in range(2):
            wait_for(block(1 - core, offset, side), sib_recv.at[side, n])
        b = lax.rem(depth + offset + y_n, y_n)
        group = pl.ds(pl.multiple_of(b * 2 * vb, 16), 2 * vb)
        prod[n] = lax.dot_general(
            panel[0, group, :], a_ref[:, :rows], NT, preferred_element_type=F32
        ) + lax.dot_general(panel[1, group, :], a_ref[:, rows:], NT, preferred_element_type=F32)
        for i in range(2):
            to = 2 * (b % 2) + i
            o = lax.rem(to - x + X, X)

            @pl.when(o == 0)
            def _():
                acc[z_of(b)] = prod[n, i * vb : (i + 1) * vb, :]

            @pl.when(o > 0)
            def _():
                code, scale = encode(prod[n, i * vb : (i + 1) * vb, :])
                xs[n, i] = code
                xs_scale[n, i] = scale
                for k, (src, dst) in ((1, (xs_scale, xr_scale)), (0, (xs, xr))):
                    pltpu.make_async_remote_copy(
                        src_ref=src.at[n, i], dst_ref=dst.at[z_of(b), o - 1], send_sem=x_send.at[k, n, i],
                        recv_sem=x_recv.at[k, z_of(b), o - 1], device_id=(prow, zh * X + to), device_id_type=MESH,
                    ).start()

    high_x = x // 2
    odd = (depth + high_x) % 2
    sign = 1 - 2 * high_x

    def reduce_x(r):
        even_way, odd_way = ((0, -1), (-2, 1), (2, -3), (4, 3))[r - 1]
        b = lax.rem(depth + sign * ((1 - odd) * even_way + odd * odd_way) + y_n, y_n)
        g = z_of(b)
        total = acc[g]
        for o in range(X - 1):
            wait_for(xr.at[g, o], x_recv.at[0, g, o])
            wait_for(xr_scale.at[g, o], x_recv.at[1, g, o])
            total = total + decode(xr[g, o], xr_scale[g, o])
        o = lax.rem(g - zh + zh_n, zh_n)
        acc[g] = total

        @pl.when(o > 0)
        def _():
            code, scale = encode(acc[g])
            zs[o - 1] = code
            zs_scale[o - 1] = scale
            for k, (src, dst) in ((1, (zs_scale, zr_scale)), (0, (zs, zr))):
                pltpu.make_async_remote_copy(
                    src_ref=src.at[o - 1], dst_ref=dst.at[o - 1], send_sem=z_send.at[k, o - 1],
                    recv_sem=z_recv.at[k, o - 1], device_id=(prow, g * X + x), device_id_type=MESH,
                ).start()

    take_pair(0)
    for o in range(1, zh_n):
        pass_local(o)
    for offset in (-1, 1):
        take_y(offset)
        spread(offset)
    for offset in (-2, 2):
        take_y(offset)
        along_y(offset, 3 if offset > 0 else -3, away[-offset // 2])
    far = 1 - 2 * core
    index = lax.rem(depth - 2 * far + y_n, y_n) * 2 + parity
    across_ring = panel.at[core, pl.ds(pl.multiple_of(index * vb, 16), vb), :]
    send(across_ring, across_ring, y_send.at[7], y_recv.at[7], (row_of(y + 2 * far, zl, core), q))
    for offset in (-2, 2):
        spread(offset)
    load_a.wait()
    multiply(0)
    for offset in (-1, 1):
        take_pair(offset)
        multiply(offset)
    for offset in (-3, 3, 4):
        take_y(offset)
        spread(offset)
    for r in (2, 3):
        for offset in (-r, r):
            take_pair(offset)
        for offset in (-r, r):
            multiply(offset)
    reduce_x(1)
    take_pair(4)
    multiply(4)
    reduce_x(2)
    reduce_x(3)

    for o in range(zh_n):
        for i in range(1, X):
            wait_for(
                piece(lax.rem(zh - o + zh_n, zh_n) * X + lax.rem(x - i + X, X)), lx_recv.at[o, i - 1]
            )
    for s in range(SNODES):
        for k in range(0, nq, 2):
            pieces = [local[(k + i) * vb : (k + i + 1) * vb, :].astype(F32) for i in range(2)]
            both = jnp.concatenate([part[s * wide : (s + 1) * wide] for part in pieces], axis=0)
            sorted_panel[s, k * wide : (k + 2) * wide, :] = both.astype(BF16)

    reduce_x(4)
    total = acc[zh]
    for o in range(zh_n - 1):
        wait_for(zr.at[o], z_recv.at[0, o])
        wait_for(zr_scale.at[o], z_recv.at[1, o])
        total = total + decode(zr[o], zr_scale[o])
    sel = -(total * mask)
    for s in range(SNODES):
        sel_ref[s] = sel[s * wide : (s + 1) * wide]

    high = sel.astype(BF16)
    low = (sel - high.astype(F32)).astype(BF16)
    for s in range(SNODES):
        part = slice(s * wide, (s + 1) * wide)
        term = lax.dot_general(high[part], sorted_panel[s], NT, preferred_element_type=F32) + lax.dot_general(
            low[part], sorted_panel[s], NT, preferred_element_type=F32
        )
        for i in range(wide // 8):
            for k in range(tiles_across):
                dpart[(s * (wide // 8) + i) * tiles_across + k] = term[i * 8 : i * 8 + 8, k * 128 : k * 128 + 128]

    chips = rows_n // 2
    number = p + chips * core

    def handler(j):
        return lax.rem(j, chips) * 2 + j // chips

    def scatter(j, carry):
        there = handler(j)

        @pl.when(there == prow)
        def _():
            pltpu.make_async_copy(dpart.at[j], dsum_in.at[prow], rs_recv.at[prow]).start()

        @pl.when(there != prow)
        def _():
            pltpu.make_async_remote_copy(
                src_ref=dpart.at[j], dst_ref=dsum_in.at[prow], send_sem=rs_send.at[j],
                recv_sem=rs_recv.at[prow], device_id=(there, q), device_id_type=MESH,
            ).start()

        return carry

    lax.fori_loop(0, tiles, scatter, 0)

    @pl.when(number < tiles)
    def _():
        def take(k, carry):
            wait_for(dsum_in.at[k], rs_recv.at[k])
            return carry

        lax.fori_loop(0, rows_n, take, 0)
        dtile[...] = jnp.sum(dsum_in[...], axis=0)

        def give(i, carry):
            @pl.when(i == prow)
            def _():
                pltpu.make_async_copy(dtile, dfin.at[number], ag_recv.at[number]).start()

            @pl.when(i != prow)
            def _():
                pltpu.make_async_remote_copy(
                    src_ref=dtile, dst_ref=dfin.at[number], send_sem=ag_send.at[i],
                    recv_sem=ag_recv.at[number], device_id=(i, q), device_id_type=MESH,
                ).start()

            return carry

        lax.fori_loop(0, rows_n, give, 0)

    def collect(j, carry):
        wait_for(dfin.at[j], ag_recv.at[j])
        return carry

    lax.fori_loop(0, tiles, collect, 0)
    for s in range(SNODES):
        for i in range(wide // 8):
            for k in range(tiles_across):
                here = (s, slice(i * 8, i * 8 + 8), slice(k * 128, k * 128 + 128))
                diag_ref[here] = dfin[(s * (wide // 8) + i) * tiles_across + k]

    for copy in started:
        copy.wait_send()

    @pl.when(jnp.logical_not(is_self))
    def _():
        wait_for(own, h_send)

    for offset in offsets:
        n = number_of[offset]
        b = lax.rem(depth + offset + y_n, y_n)
        for i in range(2):
            @pl.when(2 * (b % 2) + i != x)
            def _():
                wait_for(xs.at[n, i], x_send.at[0, n, i])
                wait_for(xs_scale.at[n, i], x_send.at[1, n, i])

    for o in range(zh_n - 1):
        wait_for(zs.at[o], z_send.at[0, o])
        wait_for(zs_scale.at[o], z_send.at[1, o])

    def scatter_done(j, carry):
        @pl.when(handler(j) != prow)
        def _():
            wait_for(dpart.at[j], rs_send.at[j])

        return carry

    lax.fori_loop(0, tiles, scatter_done, 0)

    @pl.when(number < tiles)
    def _():
        def give_done(i, carry):
            @pl.when(i != prow)
            def _():
                wait_for(dtile, ag_send.at[i])

            return carry

        lax.fori_loop(0, rows_n, give_done, 0)


def body(rows_n, cols_n, inverse_blocks, lower_panel, diag_inverse, structure):
    panel_t = jnp.swapaxes(lower_panel, 1, 2)
    snodes, wide, rows = panel_t.shape
    vb = snodes * wide
    order = diag_inverse.shape[1]
    zh_n = cols_n // X
    y_n = rows_n // 4
    tiles = (vb // 8) * (order // 128)
    vmem = pl.BlockSpec(memory_space=pltpu.VMEM)
    dma = pltpu.SemaphoreType.DMA
    hbm = pl.BlockSpec(memory_space=pltpu.HBM)
    sel_t, diag_t = pl.pallas_call(
        functools.partial(kernel, rows_n, cols_n),
        out_shape=(
            jax.ShapeDtypeStruct((snodes, wide, rows), F32),
            jax.ShapeDtypeStruct((snodes, wide, order), F32),
        ),
        in_specs=[hbm, vmem, vmem],
        out_specs=(vmem, vmem),
        scratch_shapes=[
            pltpu.VMEM(inverse_blocks.shape, BF16),
            pltpu.VMEM((2, cols_n * vb, rows), BF16),
            pltpu.VMEM((cols_n * vb, rows), BF16),
            pltpu.VMEM((y_n, 2 * vb, rows), F32),
            pltpu.VMEM((y_n, 2, vb, rows), I16),
            pltpu.VMEM((y_n, 2, 1, rows), F32),
            pltpu.VMEM((zh_n, X - 1, vb, rows), I16),
            pltpu.VMEM((zh_n, X - 1, 1, rows), F32),
            pltpu.VMEM((zh_n, vb, rows), F32),
            pltpu.VMEM((zh_n - 1, vb, rows), I16),
            pltpu.VMEM((zh_n - 1, 1, rows), F32),
            pltpu.VMEM((zh_n - 1, vb, rows), I16),
            pltpu.VMEM((zh_n - 1, 1, rows), F32),
            pltpu.VMEM((snodes, order, rows), BF16),
            pltpu.VMEM((tiles, 8, 128), F32),
            pltpu.VMEM((rows_n, 8, 128), F32),
            pltpu.VMEM((8, 128), F32),
            pltpu.VMEM((tiles, 8, 128), F32),
            dma,
            dma,
            dma,
            dma((y_n,)),
            dma((y_n,)),
            dma((y_n,)),
            dma((y_n,)),
            dma((2, y_n)),
            dma((2, y_n)),
            dma((zh_n - 1,)),
            dma((zh_n - 1,)),
            dma((zh_n, X - 1)),
            dma((zh_n, X - 1)),
            dma((2, y_n, 2)),
            dma((2, zh_n, X - 1)),
            dma((2, zh_n - 1)),
            dma((2, zh_n - 1)),
            dma((tiles,)),
            dma((rows_n,)),
            dma((rows_n,)),
            dma((tiles,)),
        ],
        compiler_params=pltpu.CompilerParams(
            collective_id=0, has_side_effects=True, vmem_limit_bytes=53 * 1024 * 1024
        ),
    )(inverse_blocks, panel_t, structure)
    return jnp.swapaxes(sel_t, 1, 2), diag_inverse - jnp.swapaxes(diag_t, 1, 2)


def solution(mesh):
    in_specs = (P("prow", "pcol"), P(None, "prow", "pcol"), P(None, None, "pcol"), P())
    out_specs = (P(None, "prow", "pcol"), P(None, None, "pcol"))
    step = functools.partial(body, mesh.shape["prow"], mesh.shape["pcol"])
    return jax.shard_map(step, mesh=mesh, in_specs=in_specs, out_specs=out_specs, check_vma=False)
```
